32 devices in a mesh: fsdp: 4 (over y, x), seq: 8 (over z, core).
Axes of the slice: x: 2, y: 2, z: 4, core: 2. Of those that a mesh axis runs over, the one named last changes fastest.
Arguments:
- tokens: bfloat16 [8192, 2048], P(('fsdp', 'seq')), may hold values from -6 to 6
- seq_lengths: int32 [4, 4], P('fsdp'), may hold values from 1 to 1024, 2048 in all within a row
- in_weight: bfloat16 [2048, 6144], P(None, 'fsdp'), may hold values from -0.125 to 0.125
- short_filter: float32 [7, 6144], replicated, may hold values from -2.5 to 2.5
- long_filter: bfloat16 [128, 128], replicated, may hold values from -0.5 to 0.5
- out_weight: bfloat16 [2048, 2048], replicated, may hold values from -0.125 to 0.125
Outputs:
- mixed: bfloat16 [8192, 2048], P(('fsdp', 'seq'))
The draws below stay inside these ranges and needn't reach their ends.
Inputs may be any that keep to these rules, and one draw needn't show every extreme that they name: `seq_lengths`: in each pack the 4 lengths sum to 2048 and the longest is exactly 1024.
All inputs are finite; a program needn't handle non-finite values.
Results may differ from the reference program's by a relative error of at most 0.0073.
Values may be sent and summed in bfloat16 or wider, within the bound.
A program may use at most 128 MiB of HBM per device.

```python
import math
import jax
import jax.numpy as jnp
import numpy as np
from jax import lax

D = 2048
GROUPS = 128
WIDTH = 7
FL = 128
SEQS = 4
GROUP = 2048
MOST = 1024
TOKENS = 8192
N_FSDP = 4


def block_scale(stream_key, extent, split, smallest, largest):
    gain = 1.0
    for dim, blocks in split:
        draws = jax.random.uniform(jax.random.fold_in(jax.random.fold_in(stream_key, 6), dim), (blocks,), jnp.float32, smallest / len(split), largest / len(split))
        gain = gain * jnp.repeat(jnp.exp(draws), extent[dim] // blocks).reshape((-1,) + (1,) * (len(extent) - 1 - dim))
    return gain


def split_up(number_of, total, reach, skew):
    loads = [(1 << 20) // math.isqrt(rank ** skew) + 1 for rank in range(2, number_of + 1)]
    surplus, given = total - reach - (number_of - 1), [1] * (number_of - 1)
    while surplus > 0:
        candidates = [i for i in range(number_of - 1) if given[i] < reach]
        pool, remaining = sum([loads[i] for i in candidates]), surplus
        for i in candidates:
            more = min(reach - given[i], max(1, remaining * loads[i] // pool), surplus)
            given[i] = given[i] + more
            surplus = surplus - more
    return np.array([reach] + given)


def uneven_parts(stream_key, count, total, reach, lean):
    if count == 2:
        one = jax.random.randint(stream_key, (), max(1, total - reach), min(reach, total - 1) + 1)
        return jnp.stack([one, total - one])
    lengths = jnp.asarray(split_up(count, total, reach, lean), jnp.int32)
    couples = (count - 1) // 2
    source_of, taker = lengths[1:1 + 2 * couples:2], lengths[2:2 + 2 * couples:2]
    margin = jnp.minimum(source_of - 1, reach - taker)
    passed = jax.random.randint(jax.random.fold_in(stream_key, 1), (couples,), 0, 1 << 20) % (margin + 1)
    lengths = lengths.at[1:1 + 2 * couples:2].set(source_of - passed).at[2:2 + 2 * couples:2].set(taker + passed)
    return lengths[jax.random.permutation(jax.random.fold_in(stream_key, 2), count)]


def noise(own_key, extent, deviation, most, pieces=(), kind=jnp.bfloat16):
    values = deviation * jax.random.normal(own_key, extent, jnp.float32)
    if pieces:
        values = values * block_scale(own_key, extent, pieces, -0.22, 0.18)
    return jnp.clip(values, -most, most).astype(kind)


def setup_inputs(seed: int = 0) -> dict:
    seeds = jax.random.split(jax.random.key(seed), 7)
    return {
        "tokens": noise(seeds[0], (TOKENS, D), 1.0, 6.0, ((0, 32),)),
        "seq_lengths": jax.vmap(lambda own: uneven_parts(own, SEQS, GROUP, MOST, 1))(jax.random.split(seeds[1], N_FSDP)).reshape((N_FSDP, SEQS)).astype(jnp.int32),
        "in_weight": noise(seeds[2], (D, 3 * D), D ** -0.5, 0.125, ((1, 4),)),
        "short_filter": noise(seeds[3], (WIDTH, 3 * D), 0.4, 2.5, (), jnp.float32),
        "long_filter": noise(seeds[4], (FL, GROUPS), FL ** -0.5, 0.5),
        "out_weight": noise(seeds[5], (D, D), D ** -0.5, 0.125),
    }


def filter_block(long_filter, window, position):
    filter_len, group_count = long_filter.shape
    out_rows = jnp.arange(filter_len, dtype=jnp.int32)[:, None]
    src_rows = jnp.arange(2 * filter_len - 1, dtype=jnp.int32)[None, :]
    tap_index = out_rows + (filter_len - 1) - src_rows
    inside = (tap_index >= 0) & (tap_index <= filter_len - 1) & (tap_index <= position[:, None])
    clipped = jnp.clip(tap_index, 0, filter_len - 1)
    kernel_table = jnp.where(inside[:, :, None], long_filter[clipped].astype(jnp.float32), 0.0).astype(jnp.float32)
    channels = window.shape[1]
    grouped = window.astype(jnp.float32).reshape(2 * filter_len - 1, group_count, channels // group_count)
    filtered = jnp.einsum("ijg,jgc->igc", kernel_table, grouped, precision=lax.Precision.HIGHEST)
    return filtered.reshape(filter_len, channels)


def reference(tokens, seq_lengths, in_weight, short_filter, long_filter, out_weight):
    projected = jnp.dot(tokens, in_weight, preferred_element_type=jnp.float32).astype(jnp.bfloat16)
    projected = projected.reshape(N_FSDP, GROUP, 3 * D)
    seq_starts = (jnp.cumsum(seq_lengths, axis=1) - seq_lengths).astype(jnp.int32)
    row_ids = jnp.arange(GROUP, dtype=jnp.int32)
    seq_begin = jnp.max(jnp.where(seq_starts[:, None, :] <= row_ids[None, :, None], seq_starts[:, None, :], 0), axis=2).astype(jnp.int32)
    position = row_ids[None, :] - seq_begin
    featured = jnp.zeros((N_FSDP, GROUP, 3 * D), jnp.float32)
    for tap_index in range(WIDTH):
        shifted = jnp.pad(projected, ((0, 0), (tap_index, 0), (0, 0)))[:, :GROUP].astype(jnp.float32)
        featured = featured + short_filter[tap_index] * jnp.where((position >= tap_index)[:, :, None], shifted, 0.0)
    queries = featured[:, :, :D]
    mixed_in = (featured[:, :, D:2 * D] * featured[:, :, 2 * D:]).astype(jnp.bfloat16)
    padded = jnp.pad(mixed_in, ((0, 0), (FL - 1, 0), (0, 0)))
    block_count = GROUP // FL

    def one_block(block_id):
        group_index = (block_id // block_count).astype(jnp.int32)
        first_row = ((block_id % block_count) * FL).astype(jnp.int32)
        window = lax.dynamic_slice(padded, (group_index, first_row, jnp.int32(0)), (1, 2 * FL - 1, D))[0]
        block_pos = lax.dynamic_slice(position, (group_index, first_row), (1, FL))[0]
        return filter_block(long_filter, window, block_pos)

    filtered = lax.map(one_block, jnp.arange(N_FSDP * block_count, dtype=jnp.int32))
    filtered = filtered.reshape(N_FSDP, GROUP, D)
    gated_out = (queries * filtered).astype(jnp.bfloat16).reshape(TOKENS, D)
    result = tokens.astype(jnp.float32) + jnp.dot(gated_out, out_weight, preferred_element_type=jnp.float32)
    return result.astype(jnp.bfloat16)
```

```python
import functools

import jax
import jax.numpy as jnp
from jax import lax
from jax.experimental import pallas as pl
from jax.experimental.pallas import tpu as pltpu
from jax.sharding import PartitionSpec as P


def from_behind(block, axis, distance):
    devices = range(lax.axis_size(axis))
    route = [(i - distance, i) for i in devices if i - distance in devices]
    return lax.ppermute(block, axis, route)


def positions(row_ids, seq_starts):
    seq_begin = jnp.max(
        jnp.where(seq_starts[None, :] <= row_ids[:, None], seq_starts[None, :], 0), axis=1
    )
    return row_ids - seq_begin


def featurize(extended, position, taps):
    width = taps.shape[0]
    rows = position.shape[0]
    total = jnp.zeros((rows, extended.shape[1]), jnp.float32)
    for tap_index in range(width):
        part = extended[width - 1 - tap_index : width - 1 - tap_index + rows].astype(jnp.float32)
        total = total + taps[tap_index] * jnp.where((position >= tap_index)[:, None], part, 0.0)
    return total


def tap_table(tap_ids, long_filter):
    filter_len = long_filter.shape[0]
    one_hot = (
        tap_ids[:, :, None] == jnp.arange(filter_len, dtype=jnp.int32)[None, None, :]
    ).astype(jnp.bfloat16)
    return jnp.einsum(
        "ijt,tg->ijg", one_hot, long_filter, preferred_element_type=jnp.float32
    ).astype(jnp.bfloat16)


def local(tokens, seq_lengths, in_weight, short_filter, long_filter, out_weight):
    row_count, channels = tokens.shape
    width = short_filter.shape[0]
    filter_len, group_count = long_filter.shape
    projected = jnp.dot(
        tokens,
        lax.all_gather(in_weight, "fsdp", axis=1, tiled=True),
        preferred_element_type=jnp.float32,
    ).astype(jnp.bfloat16)
    lengths_row = seq_lengths[0]
    seq_starts = jnp.cumsum(lengths_row) - lengths_row
    first_global = lax.axis_index("seq") * row_count
    row_ids = first_global + jnp.arange(row_count, dtype=jnp.int32)
    position = positions(row_ids, seq_starts)
    prev_tail = from_behind(projected[row_count - (width - 1) :], "seq", 1)
    extended = jnp.concatenate([prev_tail, projected], axis=0)
    featured = featurize(extended, position, short_filter)
    queries = featured[:, :channels]
    mixed_in = (featured[:, channels : 2 * channels] * featured[:, 2 * channels :]).astype(
        jnp.bfloat16
    )
    conv_tail = from_behind(mixed_in[row_count - (filter_len - 1) :], "seq", 1)
    window_all = jnp.concatenate([conv_tail, mixed_in], axis=0)
    out_rows = jnp.arange(filter_len, dtype=jnp.int32)[:, None]
    cur_tap = out_rows - jnp.arange(filter_len, dtype=jnp.int32)[None, :]
    prev_tap = out_rows + (filter_len - 1) - jnp.arange(filter_len - 1, dtype=jnp.int32)[None, :]
    cur_table = tap_table(cur_tap, long_filter)
    prev_table = tap_table(prev_tap, long_filter)
    per_group = channels // group_count
    pieces = []
    for block_id in range(row_count // filter_len):
        first_row = block_id * filter_len
        block_pos = position[first_row : first_row + filter_len]
        cur_kernel = jnp.where((cur_tap <= block_pos[:, None])[:, :, None], cur_table, 0.0)
        prev_kernel = jnp.where((prev_tap <= block_pos[:, None])[:, :, None], prev_table, 0.0)
        prev_src = window_all[first_row : first_row + filter_len - 1].reshape(
            filter_len - 1, group_count, per_group
        )
        cur_src = window_all[first_row + filter_len - 1 : first_row + 2 * filter_len - 1].reshape(
            filter_len, group_count, per_group
        )
        block_out = jnp.einsum(
            "ijg,jgc->igc", cur_kernel, cur_src, preferred_element_type=jnp.float32
        )
        block_out = block_out + jnp.einsum(
            "ijg,jgc->igc", prev_kernel, prev_src, preferred_element_type=jnp.float32
        )
        pieces.append(block_out.reshape(filter_len, channels))
    filtered = jnp.concatenate(pieces, axis=0)
    gated_out = (queries * filtered).astype(jnp.bfloat16)
    result = tokens.astype(jnp.float32) + jnp.dot(
        gated_out, out_weight, preferred_element_type=jnp.float32
    )
    return result.astype(jnp.bfloat16)


def role_kernel(tok_ref, own_ref, xm_ref, xo_ref, ym_ref, yo_ref, out_ref):
    f = lax.axis_index("fsdp")
    core = lax.rem(lax.axis_index("seq"), 2)
    half = xm_ref.shape[1]
    own_role = jnp.where(f == 0, 0, jnp.where(f == 3, 2, 1))
    x_role = jnp.where(f == 1, 0, jnp.where(f == 2, 2, 1))
    y_role = jnp.where(f < 2, 2, 0)
    tok = tok_ref[...]

    def put(role, column, weight):
        columns = pl.ds(pl.multiple_of(column, half), half)
        out_ref[role, :, columns] = jnp.dot(
            tok, weight, preferred_element_type=jnp.float32
        ).astype(jnp.bfloat16)

    put(own_role, 0, own_ref[:, :half])
    put(own_role, half, own_ref[:, half:])
    mine, other = core * half, (1 - core) * half
    put(x_role, mine, xm_ref[...])
    put(x_role, other, xo_ref[...])
    put(y_role, mine, ym_ref[...])
    put(y_role, other, yo_ref[...])


def project(tok, blocks):
    rows, block = tok.shape[0], blocks[0].shape[1]
    return pl.pallas_call(
        role_kernel,
        out_shape=jax.ShapeDtypeStruct((3, rows, block), jnp.bfloat16),
        in_specs=[pl.BlockSpec(memory_space=pltpu.VMEM)] * 6,
        out_specs=pl.BlockSpec(memory_space=pltpu.VMEM),
        compiler_params=pltpu.CompilerParams(vmem_limit_bytes=40 << 20),
        cost_estimate=pl.CostEstimate(
            flops=2 * rows * tok.shape[1] * 3 * block,
            bytes_accessed=2 * (tok.size + 3 * tok.shape[1] * block + 3 * rows * block),
            transcendentals=0,
        ),
    )(tok, *blocks)


def table_kernel(taps_ref, table_ref):
    groups, window = taps_ref.shape
    filter_len = window // 2
    for g in range(groups):
        row = jnp.broadcast_to(taps_ref[g : g + 1, :], (filter_len, window))
        shifted = pltpu.roll(row, 0, 1, stride=1, stride_axis=0)
        table_ref[g * filter_len : (g + 1) * filter_len, :] = shifted.astype(jnp.bfloat16)


def toeplitz(taps):
    groups, window = taps.shape
    return pl.pallas_call(
        table_kernel,
        out_shape=jax.ShapeDtypeStruct((groups * window // 2, window), jnp.bfloat16),
        in_specs=[pl.BlockSpec(memory_space=pltpu.VMEM)],
        out_specs=pl.BlockSpec(memory_space=pltpu.VMEM),
        compiler_params=pltpu.CompilerParams(vmem_limit_bytes=40 << 20),
    )(taps)


def mix_kernel(width, per_group, pos_ref, halo_ref, proj_ref, taps_ref, table_ref, out_ref,
               ext_ref, mixed_ref, query_ref):
    halo, rows, channels = halo_ref.shape[1], proj_ref.shape[1], proj_ref.shape[2]
    window = table_ref.shape[1]
    fl = window // 2
    for role in range(3):
        ext_ref[role, :halo, :] = halo_ref[role].astype(jnp.float32)
        ext_ref[role, halo:, :] = proj_ref[role].astype(jnp.float32)

    def feature(role, first, lanes, pos):
        total = None
        for t in range(width):
            start = halo - fl + first - t
            part = ext_ref[role, start : start + fl, lanes]
            if t > 0:
                part = jnp.where(pos >= t, part, 0.0)
            term = taps_ref[role, t : t + 1, lanes] * part
            total = term if total is None else total + term
        return total

    for first in range(0, rows + fl, fl):
        pos = pos_ref[first : first + fl, :]
        for lane in range(0, channels, 128):
            lanes = slice(lane, lane + 128)
            both = feature(1, first, lanes, pos) * feature(2, first, lanes, pos)
            mixed_ref[first : first + fl, lanes] = both.astype(jnp.bfloat16)
            if first >= fl:
                query_ref[first - fl : first, lanes] = feature(0, first, lanes, pos)

    side = 256
    many = side // per_group
    out_row = lax.broadcasted_iota(jnp.int32, (fl, window), 0)
    source = lax.broadcasted_iota(jnp.int32, (fl, window), 1)
    lane_group = lax.broadcasted_iota(jnp.int32, (fl, side), 1) // per_group
    step = 8
    for b in range(rows // fl):
        pos = pos_ref[fl + b * fl : 2 * fl + b * fl, :]
        keep = jnp.where(source >= fl + out_row - pos, 1.0, 0.0).astype(jnp.bfloat16)
        for n in range(channels // side):
            lanes = slice(n * side, (n + 1) * side)
            src = mixed_ref[b * fl : b * fl + window, lanes]
            total = jnp.zeros((fl, side), jnp.float32)
            for g0 in range(0, many, step):
                base = (n * many + g0) * fl
                tab = table_ref[base : base + step * fl, :].reshape(step, fl, window)
                tab = (tab * keep[None]).reshape(step * fl, window)
                res = jnp.dot(tab, src, preferred_element_type=jnp.float32)
                for g in range(step):
                    total = jnp.where(lane_group == g0 + g, res[g * fl : (g + 1) * fl], total)
            out_rows = slice(b * fl, (b + 1) * fl)
            out_ref[out_rows, lanes] = (query_ref[out_rows, lanes] * total).astype(jnp.bfloat16)


def mix(pos, halo, proj, taps, table, width, per_group):
    _, rows, channels = proj.shape
    fl = table.shape[1] // 2
    return pl.pallas_call(
        functools.partial(mix_kernel, width, per_group),
        out_shape=jax.ShapeDtypeStruct((rows, channels), jnp.bfloat16),
        in_specs=[pl.BlockSpec(memory_space=pltpu.VMEM)] * 5,
        out_specs=pl.BlockSpec(memory_space=pltpu.VMEM),
        scratch_shapes=[
            pltpu.VMEM((3, halo.shape[1] + rows, channels), jnp.float32),
            pltpu.VMEM((fl + rows, channels), jnp.bfloat16),
            pltpu.VMEM((rows, channels), jnp.float32),
        ],
        compiler_params=pltpu.CompilerParams(vmem_limit_bytes=40 << 20),
        cost_estimate=pl.CostEstimate(
            flops=4 * rows * table.size // 2,
            bytes_accessed=2 * (table.size + halo.size + 4 * proj.size),
            transcendentals=0,
        ),
    )(pos, halo, proj, taps, table)


def swap(block, bit):
    return lax.ppermute(block, "fsdp", [(i, i ^ bit) for i in range(4)])


def swap_cores(block):
    return lax.ppermute(block, "seq", [(i, i ^ 1) for i in range(lax.axis_size("seq"))])


def local_four(tokens, seq_lengths, in_weight, short_filter, long_filter, out_weight):
    rows, channels = tokens.shape
    width = short_filter.shape[0]
    filter_len, group_count = long_filter.shape
    per_group = channels // group_count
    f = lax.axis_index("fsdp")
    seq = lax.axis_index("seq")
    core = seq % 2
    block = channels // 4
    half = block // 2
    groups = group_count // 4

    tok_x = swap(tokens, 1)
    tok_y = swap(tokens, 2)
    odd = f % 2
    own = lax.dynamic_slice(in_weight, (0, odd * 2 * block), (channels, block))
    x_send = lax.dynamic_slice(in_weight, (0, block + core * half), (channels, half))
    y_send = lax.dynamic_slice(in_weight, (0, (1 - odd) * 2 * block + core * half), (channels, half))
    x_mine = swap(x_send, 1)
    y_mine = swap(y_send, 2)
    x_other = swap_cores(x_mine)
    y_other = swap_cores(y_mine)
    tok_d = jnp.concatenate(
        [swap(tok_x[: rows // 2], 2), swap(tok_y[rows // 2 :], 1)], axis=0
    )
    blocks = (own, x_mine, x_other, y_mine, y_other)

    lengths = lax.all_gather(seq_lengths, "fsdp", axis=0, tiled=True)
    seq_starts = jnp.cumsum(lengths, axis=1) - lengths
    row_ids = seq * rows - filter_len + jnp.arange(rows + filter_len, dtype=jnp.int32)
    taps = lax.dynamic_slice(
        short_filter.reshape(width, 3, 4, block), (0, 0, f, 0), (width, 3, 1, block)
    )[:, :, 0].transpose(1, 0, 2)
    own_filter = lax.dynamic_slice(long_filter, (0, f * groups), (filter_len, groups))
    reverse = jnp.flip(own_filter.astype(jnp.float32), 0).T
    table = toeplitz(jnp.pad(reverse, ((0, 0), (1, filter_len - 1))))

    halo_rows = filter_len + 16
    gated = []
    for bit, tok in ((0, tokens), (1, tok_x), (2, tok_y), (3, tok_d)):
        proj = project(tok, blocks)
        halo = from_behind(proj[:, rows - halo_rows :], "seq", 1)
        starts = lax.dynamic_slice(seq_starts, (f ^ bit, 0), (1, seq_starts.shape[1]))[0]
        pos = positions(row_ids, starts)[:, None]
        out = mix(pos, halo, proj, taps, table, width, per_group)
        gated.append(out if bit == 0 else swap(out, bit))

    def rows_of(bit):
        return lax.dynamic_slice(out_weight, ((f ^ bit) * block, 0), (block, channels))

    first = jnp.concatenate(gated[:3], axis=1)
    first_weight = jnp.concatenate([rows_of(0), rows_of(1), rows_of(2)], axis=0)
    result = tokens.astype(jnp.float32) + jnp.dot(
        first, first_weight, preferred_element_type=jnp.float32
    )
    result = result + jnp.dot(gated[3], rows_of(3), preferred_element_type=jnp.float32)
    return result.astype(jnp.bfloat16)


def solution(mesh):
    in_specs = (P(("fsdp", "seq"), None), P("fsdp", None), P(None, "fsdp"), P(), P(), P())
    out_specs = P(("fsdp", "seq"), None)
    body = local_four if mesh.shape["fsdp"] == 4 and mesh.shape["seq"] % 2 == 0 else local
    return jax.shard_map(body, mesh=mesh, in_specs=in_specs, out_specs=out_specs, check_vma=False)
```

```python
import functools

import jax
import jax.numpy as jnp
from jax import lax
from jax.experimental import pallas as pl
from jax.experimental.pallas import tpu as pltpu
from jax.sharding import PartitionSpec as P


def from_behind(block, axis, distance):
    devices = range(lax.axis_size(axis))
    route = [(i - distance, i) for i in devices if i - distance in devices]
    return lax.ppermute(block, axis, route)


def positions(row_ids, seq_starts):
    seq_begin = jnp.max(
        jnp.where(seq_starts[None, :] <= row_ids[:, None], seq_starts[None, :], 0), axis=1
    )
    return row_ids - seq_begin


def featurize(extended, position, taps):
    width = taps.shape[0]
    rows = position.shape[0]
    total = jnp.zeros((rows, extended.shape[1]), jnp.float32)
    for tap_index in range(width):
        part = extended[width - 1 - tap_index : width - 1 - tap_index + rows].astype(jnp.float32)
        total = total + taps[tap_index] * jnp.where((position >= tap_index)[:, None], part, 0.0)
    return total


def tap_table(tap_ids, long_filter):
    filter_len = long_filter.shape[0]
    one_hot = (
        tap_ids[:, :, None] == jnp.arange(filter_len, dtype=jnp.int32)[None, None, :]
    ).astype(jnp.bfloat16)
    return jnp.einsum(
        "ijt,tg->ijg", one_hot, long_filter, preferred_element_type=jnp.float32
    ).astype(jnp.bfloat16)


def local(tokens, seq_lengths, in_weight, short_filter, long_filter, out_weight):
    row_count, channels = tokens.shape
    width = short_filter.shape[0]
    filter_len, group_count = long_filter.shape
    projected = jnp.dot(
        tokens,
        lax.all_gather(in_weight, "fsdp", axis=1, tiled=True),
        preferred_element_type=jnp.float32,
    ).astype(jnp.bfloat16)
    lengths_row = seq_lengths[0]
    seq_starts = jnp.cumsum(lengths_row) - lengths_row
    first_global = lax.axis_index("seq") * row_count
    row_ids = first_global + jnp.arange(row_count, dtype=jnp.int32)
    position = positions(row_ids, seq_starts)
    prev_tail = from_behind(projected[row_count - (width - 1) :], "seq", 1)
    extended = jnp.concatenate([prev_tail, projected], axis=0)
    featured = featurize(extended, position, short_filter)
    queries = featured[:, :channels]
    mixed_in = (featured[:, channels : 2 * channels] * featured[:, 2 * channels :]).astype(
        jnp.bfloat16
    )
    conv_tail = from_behind(mixed_in[row_count - (filter_len - 1) :], "seq", 1)
    window_all = jnp.concatenate([conv_tail, mixed_in], axis=0)
    out_rows = jnp.arange(filter_len, dtype=jnp.int32)[:, None]
    cur_tap = out_rows - jnp.arange(filter_len, dtype=jnp.int32)[None, :]
    prev_tap = out_rows + (filter_len - 1) - jnp.arange(filter_len - 1, dtype=jnp.int32)[None, :]
    cur_table = tap_table(cur_tap, long_filter)
    prev_table = tap_table(prev_tap, long_filter)
    per_group = channels // group_count
    pieces = []
    for block_id in range(row_count // filter_len):
        first_row = block_id * filter_len
        block_pos = position[first_row : first_row + filter_len]
        cur_kernel = jnp.where((cur_tap <= block_pos[:, None])[:, :, None], cur_table, 0.0)
        prev_kernel = jnp.where((prev_tap <= block_pos[:, None])[:, :, None], prev_table, 0.0)
        prev_src = window_all[first_row : first_row + filter_len - 1].reshape(
            filter_len - 1, group_count, per_group
        )
        cur_src = window_all[first_row + filter_len - 1 : first_row + 2 * filter_len - 1].reshape(
            filter_len, group_count, per_group
        )
        block_out = jnp.einsum(
            "ijg,jgc->igc", cur_kernel, cur_src, preferred_element_type=jnp.float32
        )
        block_out = block_out + jnp.einsum(
            "ijg,jgc->igc", prev_kernel, prev_src, preferred_element_type=jnp.float32
        )
        pieces.append(block_out.reshape(filter_len, channels))
    filtered = jnp.concatenate(pieces, axis=0)
    gated_out = (queries * filtered).astype(jnp.bfloat16)
    result = tokens.astype(jnp.float32) + jnp.dot(
        gated_out, out_weight, preferred_element_type=jnp.float32
    )
    return result.astype(jnp.bfloat16)


def role_kernel(n, *refs):
    toks, weights, out_ref, tail_ref = refs[: 2 * n], refs[2 * n : -2], refs[-2], refs[-1]
    own_ref, xm_ref, xo_ref, ym_ref, yo_ref = weights
    f = lax.axis_index("fsdp")
    core = lax.rem(lax.axis_index("seq"), 2)
    half = xm_ref.shape[1]
    own_role = jnp.where(f == 0, 0, jnp.where(f == 3, 2, 1))
    x_role = jnp.where(f == 1, 0, jnp.where(f == 2, 2, 1))
    y_role = jnp.where(f < 2, 2, 0)
    rows = out_ref.shape[2]
    tok = jnp.concatenate([ref[...] for ref in toks], axis=0)
    tail = tail_ref.shape[2]

    def put(role, column, weight):
        columns = pl.ds(pl.multiple_of(column, half), half)
        made = jnp.dot(tok, weight, preferred_element_type=jnp.float32).astype(jnp.bfloat16)
        for p in range(n):
            out_ref[p, role, :, columns] = made[p * rows : (p + 1) * rows]
            tail_ref[p, role, :, columns] = made[(p + 1) * rows - tail : (p + 1) * rows]

    put(own_role, 0, own_ref[:, :half])
    put(own_role, half, own_ref[:, half:])
    mine, other = core * half, (1 - core) * half
    put(x_role, mine, xm_ref[...])
    put(x_role, other, xo_ref[...])
    put(y_role, mine, ym_ref[...])
    put(y_role, other, yo_ref[...])


def project(toks, blocks, tail):
    n = len(toks) // 2
    rows, block = 2 * toks[0].shape[0], blocks[0].shape[1]
    depth = toks[0].shape[1]
    return pl.pallas_call(
        functools.partial(role_kernel, n),
        out_shape=[
            jax.ShapeDtypeStruct((n, 3, rows, block), jnp.bfloat16),
            jax.ShapeDtypeStruct((n, 3, tail, block), jnp.bfloat16),
        ],
        in_specs=[pl.BlockSpec(memory_space=pltpu.VMEM)] * (2 * n + 5),
        out_specs=[pl.BlockSpec(memory_space=pltpu.VMEM)] * 2,
        compiler_params=pltpu.CompilerParams(vmem_limit_bytes=40 << 20),
        cost_estimate=pl.CostEstimate(
            flops=2 * n * rows * depth * 3 * block,
            bytes_accessed=2 * (n * rows * depth + 3 * depth * block + 5 * n * rows * block),
            transcendentals=0,
        ),
    )(*toks, *blocks)


def table_kernel(taps_ref, table_ref):
    groups, window = taps_ref.shape
    filter_len = window // 2
    for g in range(groups):
        row = jnp.broadcast_to(taps_ref[g : g + 1, :], (filter_len, window))
        shifted = pltpu.roll(row, 0, 1, stride=1, stride_axis=0)
        table_ref[g * filter_len : (g + 1) * filter_len, :] = shifted.astype(jnp.bfloat16)


def toeplitz(taps):
    groups, window = taps.shape
    return pl.pallas_call(
        table_kernel,
        out_shape=jax.ShapeDtypeStruct((groups * window // 2, window), jnp.bfloat16),
        in_specs=[pl.BlockSpec(memory_space=pltpu.VMEM)],
        out_specs=pl.BlockSpec(memory_space=pltpu.VMEM),
        compiler_params=pltpu.CompilerParams(vmem_limit_bytes=40 << 20),
    )(taps)


def mix_kernel(width, per_group, pos_all, halo_all, proj_all, taps_ref, table_ref, *refs):
    count = pos_all.shape[0]
    for p in range(count):
        mix_pack(width, per_group, pos_all.at[p], halo_all.at[p], proj_all.at[p], taps_ref,
                 table_ref, refs[p], *refs[count:])


def mix_pack(width, per_group, pos_ref, halo_ref, proj_ref, taps_ref, table_ref, out_ref,
             ext_ref, mixed_ref, query_ref):
    halo, rows, channels = halo_ref.shape[1], proj_ref.shape[1], proj_ref.shape[2]
    window = table_ref.shape[1]
    fl = window // 2
    for role in range(3):
        ext_ref[role, :halo, :] = halo_ref[role].astype(jnp.float32)
        ext_ref[role, halo:, :] = proj_ref[role].astype(jnp.float32)

    def feature(role, first, lanes, pos):
        total = None
        for t in range(width):
            start = halo - fl + first - t
            part = ext_ref[role, start : start + fl, lanes]
            if t > 0:
                part = jnp.where(pos >= t, part, 0.0)
            term = taps_ref[role, t : t + 1, lanes] * part
            total = term if total is None else total + term
        return total

    for first in range(0, rows + fl, fl):
        pos = pos_ref[first : first + fl, :]
        for lane in range(0, channels, 128):
            lanes = slice(lane, lane + 128)
            both = feature(1, first, lanes, pos) * feature(2, first, lanes, pos)
            mixed_ref[first : first + fl, lanes] = both.astype(jnp.bfloat16)
            if first >= fl:
                query_ref[first - fl : first, lanes] = feature(0, first, lanes, pos)

    side = 256
    many = side // per_group
    out_row = lax.broadcasted_iota(jnp.int32, (fl, window), 0)
    source = lax.broadcasted_iota(jnp.int32, (fl, window), 1)
    lane_group = lax.broadcasted_iota(jnp.int32, (fl, side), 1) // per_group
    step = 8
    for b in range(rows // fl):
        pos = pos_ref[fl + b * fl : 2 * fl + b * fl, :]
        keep = jnp.where(source >= fl + out_row - pos, 1.0, 0.0).astype(jnp.bfloat16)
        for n in range(channels // side):
            lanes = slice(n * side, (n + 1) * side)
            src = mixed_ref[b * fl : b * fl + window, lanes]
            total = jnp.zeros((fl, side), jnp.float32)
            for g0 in range(0, many, step):
                base = (n * many + g0) * fl
                tab = table_ref[base : base + step * fl, :].reshape(step, fl, window)
                tab = (tab * keep[None]).reshape(step * fl, window)
                res = jnp.dot(tab, src, preferred_element_type=jnp.float32)
                for g in range(step):
                    total = jnp.where(lane_group == g0 + g, res[g * fl : (g + 1) * fl], total)
            out_rows = slice(b * fl, (b + 1) * fl)
            out_ref[out_rows, lanes] = (query_ref[out_rows, lanes] * total).astype(jnp.bfloat16)


def mix(pos, halo, proj, taps, table, width, per_group):
    n, _, rows, channels = proj.shape
    fl = table.shape[1] // 2
    return pl.pallas_call(
        functools.partial(mix_kernel, width, per_group),
        out_shape=[jax.ShapeDtypeStruct((rows, channels), jnp.bfloat16)] * n,
        in_specs=[pl.BlockSpec(memory_space=pltpu.VMEM)] * 5,
        out_specs=[pl.BlockSpec(memory_space=pltpu.VMEM)] * n,
        scratch_shapes=[
            pltpu.VMEM((3, halo.shape[2] + rows, channels), jnp.float32),
            pltpu.VMEM((fl + rows, channels), jnp.bfloat16),
            pltpu.VMEM((rows, channels), jnp.float32),
        ],
        compiler_params=pltpu.CompilerParams(vmem_limit_bytes=40 << 20),
        cost_estimate=pl.CostEstimate(
            flops=2 * n * rows * table.size,
            bytes_accessed=2 * (table.size + halo.size + 4 * proj.size),
            transcendentals=0,
        ),
    )(pos, halo, proj, taps, table)


def swap(block, bit):
    return lax.ppermute(block, "fsdp", [(i, i ^ bit) for i in range(4)])


def swap_cores(block):
    return lax.ppermute(block, "seq", [(i, i ^ 1) for i in range(lax.axis_size("seq"))])


def local_four(tokens, seq_lengths, in_weight, short_filter, long_filter, out_weight):
    rows, channels = tokens.shape
    width = short_filter.shape[0]
    filter_len, group_count = long_filter.shape
    per_group = channels // group_count
    f = lax.axis_index("fsdp")
    seq = lax.axis_index("seq")
    core = seq % 2
    block = channels // 4
    half = block // 2
    groups = group_count // 4

    odd = f % 2
    own = lax.dynamic_slice(in_weight, (0, odd * 2 * block), (channels, block))
    x_send = lax.dynamic_slice(in_weight, (0, block + core * half), (channels, half))
    y_send = lax.dynamic_slice(in_weight, (0, (1 - odd) * 2 * block + core * half), (channels, half))
    x_mine = swap(x_send, 1)
    y_mine = swap(y_send, 2)
    x_other = swap_cores(x_mine)
    y_other = swap_cores(y_mine)
    low, high = tokens[: rows // 2], tokens[rows // 2 :]
    to_x = lax.optimization_barrier((low, high, x_mine))
    to_y = lax.optimization_barrier((high, low, y_mine))
    x_low, y_high = swap(to_x[0], 1), swap(to_y[0], 2)
    x_high, y_low = swap(to_x[1], 1), swap(to_y[1], 2)
    blocks = (own, x_mine, x_other, y_mine, y_other)

    lengths = [seq_lengths[0]] + [swap(seq_lengths, bit)[0] for bit in (1, 2, 3)]
    row_ids = seq * rows - filter_len + jnp.arange(rows + filter_len, dtype=jnp.int32)
    taps = lax.dynamic_slice(
        short_filter.reshape(width, 3, 4, block), (0, 0, f, 0), (width, 3, 1, block)
    )[:, :, 0].transpose(1, 0, 2)
    own_filter = lax.dynamic_slice(long_filter, (0, f * groups), (filter_len, groups))
    reverse = jnp.flip(own_filter.astype(jnp.float32), 0).T
    table = toeplitz(jnp.pad(reverse, ((0, 0), (1, filter_len - 1))))

    halo_rows = filter_len + 16

    def position_of(bit):
        return positions(row_ids, jnp.cumsum(lengths[bit]) - lengths[bit])[:, None]

    def mix_packs(bits, proj, halo):
        pos = jnp.stack([position_of(bit) for bit in bits])
        return mix(pos, halo, proj, taps, table, width, per_group)

    def rows_of(bit):
        return lax.dynamic_slice(out_weight, ((f ^ bit) * block, 0), (block, channels))

    proj_own, tail = project((low, high), blocks, halo_rows)
    halo_own = from_behind(tail, "seq", 1)
    to_d = lax.optimization_barrier((x_low, y_high, tail))
    d_low, d_high = swap(to_d[0], 2), swap(to_d[1], 1)
    (own_out,) = mix_packs((0,), proj_own, halo_own)
    first_weight = jnp.concatenate([rows_of(0), rows_of(1), rows_of(2)], axis=0)
    others = lax.optimization_barrier((x_low, x_high, y_low, y_high, own_out, first_weight))
    first_weight = others[5]
    proj_xy, tail_xy = project(others[:4], blocks, halo_rows)
    halo_xy = from_behind(tail_xy, "seq", 1)
    last = lax.optimization_barrier((d_low, d_high, tail_xy))
    proj_d, tail_d = project(last[:2], blocks, halo_rows)
    halo_d = from_behind(tail_d, "seq", 1)
    x_out, y_out = mix_packs((1, 2), *lax.optimization_barrier((proj_xy, halo_xy, tail_d))[:2])
    proj_d, halo_d, _ = lax.optimization_barrier((proj_d, halo_d, x_out))
    (d_out,) = mix_packs((3,), proj_d, halo_d)
    gated = [own_out, swap(x_out, 1), swap(y_out, 2), swap(d_out, 3)]

    first = jnp.concatenate(gated[:3], axis=1)
    result = tokens.astype(jnp.float32) + jnp.dot(
        first, first_weight, preferred_element_type=jnp.float32
    )
    result = result + jnp.dot(gated[3], rows_of(3), preferred_element_type=jnp.float32)
    return result.astype(jnp.bfloat16)


def solution(mesh):
    in_specs = (P(("fsdp", "seq"), None), P("fsdp", None), P(None, "fsdp"), P(), P(), P())
    out_specs = P(("fsdp", "seq"), None)
    body = local_four if mesh.shape["fsdp"] == 4 and mesh.shape["seq"] % 2 == 0 else local
    return jax.shard_map(body, mesh=mesh, in_specs=in_specs, out_specs=out_specs, check_vma=False)
```

```python
import functools

import jax
import jax.numpy as jnp
from jax import lax
from jax.experimental import pallas as pl
from jax.experimental.pallas import tpu as pltpu
from jax.sharding import PartitionSpec as P


def from_behind(block, axis, distance):
    devices = range(lax.axis_size(axis))
    route = [(i - distance, i) for i in devices if i - distance in devices]
    return lax.ppermute(block, axis, route)


def positions(row_ids, seq_starts):
    seq_begin = jnp.max(
        jnp.where(seq_starts[None, :] <= row_ids[:, None], seq_starts[None, :], 0), axis=1
    )
    return row_ids - seq_begin


def featurize(extended, position, taps):
    width = taps.shape[0]
    rows = position.shape[0]
    total = jnp.zeros((rows, extended.shape[1]), jnp.float32)
    for tap_index in range(width):
        part = extended[width - 1 - tap_index : width - 1 - tap_index + rows].astype(jnp.float32)
        total = total + taps[tap_index] * jnp.where((position >= tap_index)[:, None], part, 0.0)
    return total


def tap_table(tap_ids, long_filter):
    filter_len = long_filter.shape[0]
    one_hot = (
        tap_ids[:, :, None] == jnp.arange(filter_len, dtype=jnp.int32)[None, None, :]
    ).astype(jnp.bfloat16)
    return jnp.einsum(
        "ijt,tg->ijg", one_hot, long_filter, preferred_element_type=jnp.float32
    ).astype(jnp.bfloat16)


def local(tokens, seq_lengths, in_weight, short_filter, long_filter, out_weight):
    row_count, channels = tokens.shape
    width = short_filter.shape[0]
    filter_len, group_count = long_filter.shape
    projected = jnp.dot(
        tokens,
        lax.all_gather(in_weight, "fsdp", axis=1, tiled=True),
        preferred_element_type=jnp.float32,
    ).astype(jnp.bfloat16)
    lengths_row = seq_lengths[0]
    seq_starts = jnp.cumsum(lengths_row) - lengths_row
    first_global = lax.axis_index("seq") * row_count
    row_ids = first_global + jnp.arange(row_count, dtype=jnp.int32)
    position = positions(row_ids, seq_starts)
    prev_tail = from_behind(projected[row_count - (width - 1) :], "seq", 1)
    extended = jnp.concatenate([prev_tail, projected], axis=0)
    featured = featurize(extended, position, short_filter)
    queries = featured[:, :channels]
    mixed_in = (featured[:, channels : 2 * channels] * featured[:, 2 * channels :]).astype(
        jnp.bfloat16
    )
    conv_tail = from_behind(mixed_in[row_count - (filter_len - 1) :], "seq", 1)
    window_all = jnp.concatenate([conv_tail, mixed_in], axis=0)
    out_rows = jnp.arange(filter_len, dtype=jnp.int32)[:, None]
    cur_tap = out_rows - jnp.arange(filter_len, dtype=jnp.int32)[None, :]
    prev_tap = out_rows + (filter_len - 1) - jnp.arange(filter_len - 1, dtype=jnp.int32)[None, :]
    cur_table = tap_table(cur_tap, long_filter)
    prev_table = tap_table(prev_tap, long_filter)
    per_group = channels // group_count
    pieces = []
    for block_id in range(row_count // filter_len):
        first_row = block_id * filter_len
        block_pos = position[first_row : first_row + filter_len]
        cur_kernel = jnp.where((cur_tap <= block_pos[:, None])[:, :, None], cur_table, 0.0)
        prev_kernel = jnp.where((prev_tap <= block_pos[:, None])[:, :, None], prev_table, 0.0)
        prev_src = window_all[first_row : first_row + filter_len - 1].reshape(
            filter_len - 1, group_count, per_group
        )
        cur_src = window_all[first_row + filter_len - 1 : first_row + 2 * filter_len - 1].reshape(
            filter_len, group_count, per_group
        )
        block_out = jnp.einsum(
            "ijg,jgc->igc", cur_kernel, cur_src, preferred_element_type=jnp.float32
        )
        block_out = block_out + jnp.einsum(
            "ijg,jgc->igc", prev_kernel, prev_src, preferred_element_type=jnp.float32
        )
        pieces.append(block_out.reshape(filter_len, channels))
    filtered = jnp.concatenate(pieces, axis=0)
    gated_out = (queries * filtered).astype(jnp.bfloat16)
    result = tokens.astype(jnp.float32) + jnp.dot(
        gated_out, out_weight, preferred_element_type=jnp.float32
    )
    return result.astype(jnp.bfloat16)


def role_kernel(n, *refs):
    toks, weights, out_ref, tail_ref = refs[: 2 * n], refs[2 * n : -2], refs[-2], refs[-1]
    own_ref, xm_ref, xo_ref, ym_ref, yo_ref = weights
    f = lax.axis_index("fsdp")
    core = lax.rem(lax.axis_index("seq"), 2)
    half = xm_ref.shape[1]
    own_role = jnp.where(f == 0, 0, jnp.where(f == 3, 2, 1))
    x_role = jnp.where(f == 1, 0, jnp.where(f == 2, 2, 1))
    y_role = jnp.where(f < 2, 2, 0)
    rows = out_ref.shape[2]
    tok = jnp.concatenate([ref[...] for ref in toks], axis=0)
    tail = tail_ref.shape[2]

    def put(role, column, weight):
        columns = pl.ds(pl.multiple_of(column, half), half)
        made = jnp.dot(tok, weight, preferred_element_type=jnp.float32).astype(jnp.bfloat16)
        for p in range(n):
            out_ref[p, role, :, columns] = made[p * rows : (p + 1) * rows]
            tail_ref[p, role, :, columns] = made[(p + 1) * rows - tail : (p + 1) * rows]

    put(own_role, 0, own_ref[:, :half])
    put(own_role, half, own_ref[:, half:])
    mine, other = core * half, (1 - core) * half
    put(x_role, mine, xm_ref[...])
    put(x_role, other, xo_ref[...])
    put(y_role, mine, ym_ref[...])
    put(y_role, other, yo_ref[...])


def project(toks, blocks, tail):
    n = len(toks) // 2
    rows, block = 2 * toks[0].shape[0], blocks[0].shape[1]
    depth = toks[0].shape[1]
    return pl.pallas_call(
        functools.partial(role_kernel, n),
        out_shape=[
            jax.ShapeDtypeStruct((n, 3, rows, block), jnp.bfloat16),
            jax.ShapeDtypeStruct((n, 3, tail, block), jnp.bfloat16),
        ],
        in_specs=[pl.BlockSpec(memory_space=pltpu.VMEM)] * (2 * n + 5),
        out_specs=[pl.BlockSpec(memory_space=pltpu.VMEM)] * 2,
        compiler_params=pltpu.CompilerParams(vmem_limit_bytes=40 << 20),
        cost_estimate=pl.CostEstimate(
            flops=2 * n * rows * depth * 3 * block,
            bytes_accessed=2 * (n * rows * depth + 3 * depth * block + 5 * n * rows * block),
            transcendentals=0,
        ),
    )(*toks, *blocks)


def table_kernel(taps_ref, table_ref):
    groups, window = taps_ref.shape
    filter_len = window // 2
    for g in range(groups):
        row = jnp.broadcast_to(taps_ref[g : g + 1, :], (filter_len, window))
        shifted = pltpu.roll(row, 0, 1, stride=1, stride_axis=0)
        table_ref[g * filter_len : (g + 1) * filter_len, :] = shifted.astype(jnp.bfloat16)


def toeplitz(taps):
    groups, window = taps.shape
    return pl.pallas_call(
        table_kernel,
        out_shape=jax.ShapeDtypeStruct((groups * window // 2, window), jnp.bfloat16),
        in_specs=[pl.BlockSpec(memory_space=pltpu.VMEM)],
        out_specs=pl.BlockSpec(memory_space=pltpu.VMEM),
        compiler_params=pltpu.CompilerParams(vmem_limit_bytes=40 << 20),
    )(taps)


def mix_kernel(width, per_group, pos_all, halo_all, proj_all, taps_ref, table_ref, *refs):
    count = pos_all.shape[0]
    for p in range(count):
        mix_pack(width, per_group, pos_all.at[p], halo_all.at[p], proj_all.at[p], taps_ref,
                 table_ref, refs[p], *refs[count:])


def mix_pack(width, per_group, pos_ref, halo_ref, proj_ref, taps_ref, table_ref, out_ref,
             ext_ref, mixed_ref, query_ref):
    halo, rows, channels = halo_ref.shape[1], proj_ref.shape[1], proj_ref.shape[2]
    window = table_ref.shape[1]
    fl = window // 2
    for role in range(3):
        ext_ref[role, :halo, :] = halo_ref[role].astype(jnp.float32)
        ext_ref[role, halo:, :] = proj_ref[role].astype(jnp.float32)

    def feature(role, first, lanes, pos):
        total = None
        for t in range(width):
            start = halo - fl + first - t
            part = ext_ref[role, start : start + fl, lanes]
            if t > 0:
                part = jnp.where(pos >= t, part, 0.0)
            term = taps_ref[role, t : t + 1, lanes] * part
            total = term if total is None else total + term
        return total

    for first in range(0, rows + fl, fl):
        pos = pos_ref[first : first + fl, :]
        for lane in range(0, channels, 128):
            lanes = slice(lane, lane + 128)
            both = feature(1, first, lanes, pos) * feature(2, first, lanes, pos)
            mixed_ref[first : first + fl, lanes] = both.astype(jnp.bfloat16)
            if first >= fl:
                query_ref[first - fl : first, lanes] = feature(0, first, lanes, pos)

    side = 256
    many = side // per_group
    out_row = lax.broadcasted_iota(jnp.int32, (fl, window), 0)
    source = lax.broadcasted_iota(jnp.int32, (fl, window), 1)
    lane_group = lax.broadcasted_iota(jnp.int32, (fl, side), 1) // per_group
    step = 8
    for b in range(rows // fl):
        pos = pos_ref[fl + b * fl : 2 * fl + b * fl, :]
        keep = jnp.where(source >= fl + out_row - pos, 1.0, 0.0).astype(jnp.bfloat16)
        for n in range(channels // side):
            lanes = slice(n * side, (n + 1) * side)
            src = mixed_ref[b * fl : b * fl + window, lanes]
            total = jnp.zeros((fl, side), jnp.float32)
            for g0 in range(0, many, step):
                base = (n * many + g0) * fl
                tab = table_ref[base : base + step * fl, :].reshape(step, fl, window)
                tab = (tab * keep[None]).reshape(step * fl, window)
                res = jnp.dot(tab, src, preferred_element_type=jnp.float32)
                for g in range(step):
                    total = jnp.where(lane_group == g0 + g, res[g * fl : (g + 1) * fl], total)
            out_rows = slice(b * fl, (b + 1) * fl)
            out_ref[out_rows, lanes] = (query_ref[out_rows, lanes] * total).astype(jnp.bfloat16)


def mix(pos, halo, proj, taps, table, width, per_group):
    n, _, rows, channels = proj.shape
    fl = table.shape[1] // 2
    return pl.pallas_call(
        functools.partial(mix_kernel, width, per_group),
        out_shape=[jax.ShapeDtypeStruct((rows, channels), jnp.bfloat16)] * n,
        in_specs=[pl.BlockSpec(memory_space=pltpu.VMEM)] * 5,
        out_specs=[pl.BlockSpec(memory_space=pltpu.VMEM)] * n,
        scratch_shapes=[
            pltpu.VMEM((3, halo.shape[2] + rows, channels), jnp.float32),
            pltpu.VMEM((fl + rows, channels), jnp.bfloat16),
            pltpu.VMEM((rows, channels), jnp.float32),
        ],
        compiler_params=pltpu.CompilerParams(vmem_limit_bytes=40 << 20),
        cost_estimate=pl.CostEstimate(
            flops=2 * n * rows * table.size,
            bytes_accessed=2 * (table.size + halo.size + 4 * proj.size),
            transcendentals=0,
        ),
    )(pos, halo, proj, taps, table)


def swap(block, bit):
    return lax.ppermute(block, "fsdp", [(i, i ^ bit) for i in range(4)])


def swap_cores(block):
    return lax.ppermute(block, "seq", [(i, i ^ 1) for i in range(lax.axis_size("seq"))])


def local_four(tokens, seq_lengths, in_weight, short_filter, long_filter, out_weight):
    rows, channels = tokens.shape
    width = short_filter.shape[0]
    filter_len, group_count = long_filter.shape
    per_group = channels // group_count
    f = lax.axis_index("fsdp")
    seq = lax.axis_index("seq")
    core = seq % 2
    block = channels // 4
    half = block // 2
    groups = group_count // 4

    odd = f % 2
    own = lax.dynamic_slice(in_weight, (0, odd * 2 * block), (channels, block))
    x_send = lax.dynamic_slice(in_weight, (0, block + core * half), (channels, half))
    y_send = lax.dynamic_slice(in_weight, (0, (1 - odd) * 2 * block + core * half), (channels, half))
    x_mine = swap(x_send, 1)
    y_mine = swap(y_send, 2)
    x_other = swap_cores(x_mine)
    y_other = swap_cores(y_mine)
    low, high = tokens[: rows // 2], tokens[rows // 2 :]
    to_x = lax.optimization_barrier((low, high, x_mine))
    to_y = lax.optimization_barrier((high, low, y_mine))
    x_low, y_high = swap(to_x[0], 1), swap(to_y[0], 2)
    x_high, y_low = swap(to_x[1], 1), swap(to_y[1], 2)
    blocks = (own, x_mine, x_other, y_mine, y_other)

    lengths = [seq_lengths] + [swap(seq_lengths, bit) for bit in (1, 2, 3)]
    taps = lax.dynamic_slice(
        short_filter.reshape(width, 3, 4, block), (0, 0, f, 0), (width, 3, 1, block)
    )[:, :, 0].transpose(1, 0, 2)
    own_filter = lax.dynamic_slice(long_filter, (0, f * groups), (filter_len, groups))
    reverse = jnp.flip(own_filter.astype(jnp.float32), 0).T
    table = toeplitz(jnp.pad(reverse, ((0, 0), (1, filter_len - 1))))

    halo_rows = filter_len + 16

    def rows_of(bit):
        return lax.dynamic_slice(out_weight, ((f ^ bit) * block, 0), (block, channels))

    proj_own, tail = project((low, high), blocks, halo_rows)
    halo_own = from_behind(tail, "seq", 1)
    to_d = lax.optimization_barrier((x_low, y_high, tail))
    d_low, d_high = swap(to_d[0], 2), swap(to_d[1], 1)

    every = jnp.concatenate(lax.optimization_barrier((*lengths, tail))[:4], axis=0)
    ids = jnp.arange(every.shape[1], dtype=jnp.int32)
    earlier = (ids[:, None] < ids[None, :]).astype(jnp.int32)
    starts = jnp.sum(every[:, :, None] * earlier[None], axis=1)
    row_ids = seq * rows - filter_len + jnp.arange(rows + filter_len, dtype=jnp.int32)
    before = jnp.where(starts[:, None, :] <= row_ids[None, :, None], starts[:, None, :], 0)
    position = (row_ids[None, :] - jnp.max(before, axis=2))[:, :, None]

    def mix_packs(first, last, proj, halo):
        return mix(position[first:last], halo, proj, taps, table, width, per_group)

    (own_out,) = mix_packs(0, 1, proj_own, halo_own)
    weights = [rows_of(bit) for bit in range(4)]
    total = tokens.astype(jnp.float32) + jnp.dot(
        own_out, weights[0], preferred_element_type=jnp.float32
    )
    others = lax.optimization_barrier(
        (x_low, x_high, y_low, y_high, own_out, total, *weights[1:])
    )
    total, weights[1:] = others[5], others[6:]
    proj_xy, tail_xy = project(others[:4], blocks, halo_rows)
    halo_xy = from_behind(tail_xy, "seq", 1)
    last = lax.optimization_barrier((d_low, d_high, tail_xy))
    proj_d, tail_d = project(last[:2], blocks, halo_rows)
    halo_d = from_behind(tail_d, "seq", 1)
    x_out, y_out = mix_packs(1, 3, *lax.optimization_barrier((proj_xy, halo_xy, tail_d))[:2])
    proj_d, halo_d, _ = lax.optimization_barrier((proj_d, halo_d, x_out))
    (d_out,) = mix_packs(3, 4, proj_d, halo_d)
    x_back, y_back, d_back = swap(x_out, 1), swap(y_out, 2), swap(d_out, 3)
    total = total + jnp.dot(x_back, weights[1], preferred_element_type=jnp.float32)
    total = total + jnp.dot(y_back, weights[2], preferred_element_type=jnp.float32)
    (total,) = lax.optimization_barrier((total,))
    total = total + jnp.dot(d_back, weights[3], preferred_element_type=jnp.float32)
    return total.astype(jnp.bfloat16)


def solution(mesh):
    in_specs = (P(("fsdp", "seq"), None), P("fsdp", None), P(None, "fsdp"), P(), P(), P())
    out_specs = P(("fsdp", "seq"), None)
    body = local_four if mesh.shape["fsdp"] == 4 and mesh.shape["seq"] % 2 == 0 else local
    return jax.shard_map(body, mesh=mesh, in_specs=in_specs, out_specs=out_specs, check_vma=False)
```

```python
import functools

import jax
import jax.numpy as jnp
from jax import lax
from jax.experimental import pallas as pl
from jax.experimental.pallas import tpu as pltpu
from jax.sharding import PartitionSpec as P


def from_behind(block, axis, distance):
    devices = range(lax.axis_size(axis))
    route = [(i - distance, i) for i in devices if i - distance in devices]
    return lax.ppermute(block, axis, route)


def positions(row_ids, seq_starts):
    seq_begin = jnp.max(
        jnp.where(seq_starts[None, :] <= row_ids[:, None], seq_starts[None, :], 0), axis=1
    )
    return row_ids - seq_begin


def featurize(extended, position, taps):
    width = taps.shape[0]
    rows = position.shape[0]
    total = jnp.zeros((rows, extended.shape[1]), jnp.float32)
    for tap_index in range(width):
        part = extended[width - 1 - tap_index : width - 1 - tap_index + rows].astype(jnp.float32)
        total = total + taps[tap_index] * jnp.where((position >= tap_index)[:, None], part, 0.0)
    return total


def tap_table(tap_ids, long_filter):
    filter_len = long_filter.shape[0]
    one_hot = (
        tap_ids[:, :, None] == jnp.arange(filter_len, dtype=jnp.int32)[None, None, :]
    ).astype(jnp.bfloat16)
    return jnp.einsum(
        "ijt,tg->ijg", one_hot, long_filter, preferred_element_type=jnp.float32
    ).astype(jnp.bfloat16)


def local(tokens, seq_lengths, in_weight, short_filter, long_filter, out_weight):
    row_count, channels = tokens.shape
    width = short_filter.shape[0]
    filter_len, group_count = long_filter.shape
    projected = jnp.dot(
        tokens,
        lax.all_gather(in_weight, "fsdp", axis=1, tiled=True),
        preferred_element_type=jnp.float32,
    ).astype(jnp.bfloat16)
    lengths_row = seq_lengths[0]
    seq_starts = jnp.cumsum(lengths_row) - lengths_row
    first_global = lax.axis_index("seq") * row_count
    row_ids = first_global + jnp.arange(row_count, dtype=jnp.int32)
    position = positions(row_ids, seq_starts)
    prev_tail = from_behind(projected[row_count - (width - 1) :], "seq", 1)
    extended = jnp.concatenate([prev_tail, projected], axis=0)
    featured = featurize(extended, position, short_filter)
    queries = featured[:, :channels]
    mixed_in = (featured[:, channels : 2 * channels] * featured[:, 2 * channels :]).astype(
        jnp.bfloat16
    )
    conv_tail = from_behind(mixed_in[row_count - (filter_len - 1) :], "seq", 1)
    window_all = jnp.concatenate([conv_tail, mixed_in], axis=0)
    out_rows = jnp.arange(filter_len, dtype=jnp.int32)[:, None]
    cur_tap = out_rows - jnp.arange(filter_len, dtype=jnp.int32)[None, :]
    prev_tap = out_rows + (filter_len - 1) - jnp.arange(filter_len - 1, dtype=jnp.int32)[None, :]
    cur_table = tap_table(cur_tap, long_filter)
    prev_table = tap_table(prev_tap, long_filter)
    per_group = channels // group_count
    pieces = []
    for block_id in range(row_count // filter_len):
        first_row = block_id * filter_len
        block_pos = position[first_row : first_row + filter_len]
        cur_kernel = jnp.where((cur_tap <= block_pos[:, None])[:, :, None], cur_table, 0.0)
        prev_kernel = jnp.where((prev_tap <= block_pos[:, None])[:, :, None], prev_table, 0.0)
        prev_src = window_all[first_row : first_row + filter_len - 1].reshape(
            filter_len - 1, group_count, per_group
        )
        cur_src = window_all[first_row + filter_len - 1 : first_row + 2 * filter_len - 1].reshape(
            filter_len, group_count, per_group
        )
        block_out = jnp.einsum(
            "ijg,jgc->igc", cur_kernel, cur_src, preferred_element_type=jnp.float32
        )
        block_out = block_out + jnp.einsum(
            "ijg,jgc->igc", prev_kernel, prev_src, preferred_element_type=jnp.float32
        )
        pieces.append(block_out.reshape(filter_len, channels))
    filtered = jnp.concatenate(pieces, axis=0)
    gated_out = (queries * filtered).astype(jnp.bfloat16)
    result = tokens.astype(jnp.float32) + jnp.dot(
        gated_out, out_weight, preferred_element_type=jnp.float32
    )
    return result.astype(jnp.bfloat16)


def role_kernel(n, *refs):
    toks, weights, out_ref, tail_ref = refs[: 2 * n], refs[2 * n : -2], refs[-2], refs[-1]
    own_ref, xm_ref, xo_ref, ym_ref, yo_ref = weights
    f = lax.axis_index("fsdp")
    core = lax.rem(lax.axis_index("seq"), 2)
    half = xm_ref.shape[1]
    own_role = jnp.where(f == 0, 0, jnp.where(f == 3, 2, 1))
    x_role = jnp.where(f == 1, 0, jnp.where(f == 2, 2, 1))
    y_role = jnp.where(f < 2, 2, 0)
    rows = out_ref.shape[2]
    tok = jnp.concatenate([ref[...] for ref in toks], axis=0)
    tail = tail_ref.shape[2]

    def put(role, column, weight):
        columns = pl.ds(pl.multiple_of(column, half), half)
        made = jnp.dot(tok, weight, preferred_element_type=jnp.float32).astype(jnp.bfloat16)
        for p in range(n):
            out_ref[p, role, :, columns] = made[p * rows : (p + 1) * rows]
            tail_ref[p, role, :, columns] = made[(p + 1) * rows - tail : (p + 1) * rows]

    put(own_role, 0, own_ref[:, :half])
    put(own_role, half, own_ref[:, half:])
    mine, other = core * half, (1 - core) * half
    put(x_role, mine, xm_ref[...])
    put(x_role, other, xo_ref[...])
    put(y_role, mine, ym_ref[...])
    put(y_role, other, yo_ref[...])


def project(toks, blocks, tail):
    n = len(toks) // 2
    rows, block = 2 * toks[0].shape[0], blocks[0].shape[1]
    depth = toks[0].shape[1]
    return pl.pallas_call(
        functools.partial(role_kernel, n),
        out_shape=[
            jax.ShapeDtypeStruct((n, 3, rows, block), jnp.bfloat16),
            jax.ShapeDtypeStruct((n, 3, tail, block), jnp.bfloat16),
        ],
        in_specs=[pl.BlockSpec(memory_space=pltpu.VMEM)] * (2 * n + 5),
        out_specs=[pl.BlockSpec(memory_space=pltpu.VMEM)] * 2,
        compiler_params=pltpu.CompilerParams(vmem_limit_bytes=40 << 20),
        cost_estimate=pl.CostEstimate(
            flops=2 * n * rows * depth * 3 * block,
            bytes_accessed=2 * (n * rows * depth + 3 * depth * block + 5 * n * rows * block),
            transcendentals=0,
        ),
    )(*toks, *blocks)


def table_kernel(taps_ref, table_ref):
    groups, window = taps_ref.shape
    filter_len = window // 2
    for g in range(groups):
        row = jnp.broadcast_to(taps_ref[g : g + 1, :], (filter_len, window))
        shifted = pltpu.roll(row, 0, 1, stride=1, stride_axis=0)
        table_ref[g * filter_len : (g + 1) * filter_len, :] = shifted.astype(jnp.bfloat16)


def toeplitz(taps):
    groups, window = taps.shape
    return pl.pallas_call(
        table_kernel,
        out_shape=jax.ShapeDtypeStruct((groups * window // 2, window), jnp.bfloat16),
        in_specs=[pl.BlockSpec(memory_space=pltpu.VMEM)],
        out_specs=pl.BlockSpec(memory_space=pltpu.VMEM),
        compiler_params=pltpu.CompilerParams(vmem_limit_bytes=40 << 20),
    )(taps)


def mix_kernel(width, per_group, pos_all, halo_all, proj_all, taps_ref, table_ref, *refs):
    count = pos_all.shape[0]
    for p in range(count):
        mix_pack(width, per_group, pos_all.at[p], halo_all.at[p], proj_all.at[p], taps_ref,
                 table_ref, refs[p], *refs[count:])


def mix_pack(width, per_group, pos_ref, halo_ref, proj_ref, taps_ref, table_ref, out_ref,
             ext_ref, mixed_ref, query_ref):
    halo, rows, channels = halo_ref.shape[1], proj_ref.shape[1], proj_ref.shape[2]
    window = table_ref.shape[1]
    fl = window // 2
    for role in range(3):
        ext_ref[role, :halo, :] = halo_ref[role].astype(jnp.float32)
        ext_ref[role, halo:, :] = proj_ref[role].astype(jnp.float32)

    def feature(role, first, lanes, pos):
        total = None
        for t in range(width):
            start = halo - fl + first - t
            part = ext_ref[role, start : start + fl, lanes]
            if t > 0:
                part = jnp.where(pos >= t, part, 0.0)
            term = taps_ref[role, t : t + 1, lanes] * part
            total = term if total is None else total + term
        return total

    for first in range(0, rows + fl, fl):
        pos = pos_ref[first : first + fl, :]
        for lane in range(0, channels, 128):
            lanes = slice(lane, lane + 128)
            both = feature(1, first, lanes, pos) * feature(2, first, lanes, pos)
            mixed_ref[first : first + fl, lanes] = both.astype(jnp.bfloat16)
            if first >= fl:
                query_ref[first - fl : first, lanes] = feature(0, first, lanes, pos)

    side = 256
    many = side // per_group
    out_row = lax.broadcasted_iota(jnp.int32, (fl, window), 0)
    source = lax.broadcasted_iota(jnp.int32, (fl, window), 1)
    lane_group = lax.broadcasted_iota(jnp.int32, (fl, side), 1) // per_group
    step = 8
    for b in range(rows // fl):
        pos = pos_ref[fl + b * fl : 2 * fl + b * fl, :]
        keep = jnp.where(source >= fl + out_row - pos, 1.0, 0.0).astype(jnp.bfloat16)
        for n in range(channels // side):
            lanes = slice(n * side, (n + 1) * side)
            src = mixed_ref[b * fl : b * fl + window, lanes]
            total = jnp.zeros((fl, side), jnp.float32)
            for g0 in range(0, many, step):
                base = (n * many + g0) * fl
                tab = table_ref[base : base + step * fl, :].reshape(step, fl, window)
                tab = (tab * keep[None]).reshape(step * fl, window)
                res = jnp.dot(tab, src, preferred_element_type=jnp.float32)
                for g in range(step):
                    total = jnp.where(lane_group == g0 + g, res[g * fl : (g + 1) * fl], total)
            out_rows = slice(b * fl, (b + 1) * fl)
            out_ref[out_rows, lanes] = (query_ref[out_rows, lanes] * total).astype(jnp.bfloat16)


def mix(pos, halo, proj, taps, table, width, per_group):
    n, _, rows, channels = proj.shape
    fl = table.shape[1] // 2
    return pl.pallas_call(
        functools.partial(mix_kernel, width, per_group),
        out_shape=[jax.ShapeDtypeStruct((rows, channels), jnp.bfloat16)] * n,
        in_specs=[pl.BlockSpec(memory_space=pltpu.VMEM)] * 5,
        out_specs=[pl.BlockSpec(memory_space=pltpu.VMEM)] * n,
        scratch_shapes=[
            pltpu.VMEM((3, halo.shape[2] + rows, channels), jnp.float32),
            pltpu.VMEM((fl + rows, channels), jnp.bfloat16),
            pltpu.VMEM((rows, channels), jnp.float32),
        ],
        compiler_params=pltpu.CompilerParams(vmem_limit_bytes=40 << 20),
        cost_estimate=pl.CostEstimate(
            flops=2 * n * rows * table.size,
            bytes_accessed=2 * (table.size + halo.size + 4 * proj.size),
            transcendentals=0,
        ),
    )(pos, halo, proj, taps, table)


def swap(block, bit):
    return lax.ppermute(block, "fsdp", [(i, i ^ bit) for i in range(4)])


def swap_cores(block):
    return lax.ppermute(block, "seq", [(i, i ^ 1) for i in range(lax.axis_size("seq"))])


def local_four(tokens, seq_lengths, in_weight, short_filter, long_filter, out_weight):
    rows, channels = tokens.shape
    width = short_filter.shape[0]
    filter_len, group_count = long_filter.shape
    per_group = channels // group_count
    f = lax.axis_index("fsdp")
    seq = lax.axis_index("seq")
    core = seq % 2
    block = channels // 4
    half = block // 2
    groups = group_count // 4

    odd = f % 2
    own = lax.dynamic_slice(in_weight, (0, odd * 2 * block), (channels, block))
    x_send = lax.dynamic_slice(in_weight, (0, block + core * half), (channels, half))
    y_send = lax.dynamic_slice(in_weight, (0, (1 - odd) * 2 * block + core * half), (channels, half))
    x_mine = swap(x_send, 1)
    y_mine = swap(y_send, 2)
    x_other = swap_cores(x_mine)
    y_other = swap_cores(y_mine)
    low, high = tokens[: rows // 2], tokens[rows // 2 :]
    to_x = lax.optimization_barrier((low, high, x_mine))
    to_y = lax.optimization_barrier((high, low, y_mine))
    x_low, y_high = swap(to_x[0], 1), swap(to_y[0], 2)
    x_high, y_low = swap(to_x[1], 1), swap(to_y[1], 2)
    blocks = (own, x_mine, x_other, y_mine, y_other)

    lengths = [seq_lengths] + [swap(seq_lengths, bit) for bit in (1, 2, 3)]
    taps = lax.dynamic_slice(
        short_filter.reshape(width, 3, 4, block), (0, 0, f, 0), (width, 3, 1, block)
    )[:, :, 0].transpose(1, 0, 2)
    own_filter = lax.dynamic_slice(long_filter, (0, f * groups), (filter_len, groups))
    reverse = jnp.flip(own_filter.astype(jnp.float32), 0).T
    table = toeplitz(jnp.pad(reverse, ((0, 0), (1, filter_len - 1))))

    halo_rows = filter_len + 16

    proj_own, tail = project((low, high), blocks, halo_rows)
    halo_own = from_behind(tail, "seq", 1)
    late_weight = lax.optimization_barrier((out_weight, tail))[0]

    def rows_of(bit):
        return lax.dynamic_slice(late_weight, ((f ^ bit) * block, 0), (block, channels))

    every = jnp.concatenate(lax.optimization_barrier((*lengths, tail))[:4], axis=0)
    ids = jnp.arange(every.shape[1], dtype=jnp.int32)
    earlier = (ids[:, None] < ids[None, :]).astype(jnp.int32)
    starts = jnp.sum(every[:, :, None] * earlier[None], axis=1)
    row_ids = seq * rows - filter_len + jnp.arange(rows + filter_len, dtype=jnp.int32)
    before = jnp.where(starts[:, None, :] <= row_ids[None, :, None], starts[:, None, :], 0)
    position = (row_ids[None, :] - jnp.max(before, axis=2))[:, :, None]

    def mix_packs(first, last, proj, halo):
        return mix(position[first:last], halo, proj, taps, table, width, per_group)

    (own_out,) = mix_packs(0, 1, proj_own, halo_own)
    weights = [rows_of(bit) for bit in range(4)]
    to_d = lax.optimization_barrier((x_low, y_high, own_out, *weights[1:]))
    d_low, d_high = swap(to_d[0], 2), swap(to_d[1], 1)
    total = tokens.astype(jnp.float32) + jnp.dot(
        own_out, weights[0], preferred_element_type=jnp.float32
    )
    others = lax.optimization_barrier(
        (x_low, x_high, y_low, y_high, own_out, total, *weights[1:])
    )
    total, weights[1:] = others[5], others[6:]
    proj_xy, tail_xy = project(others[:4], blocks, halo_rows)
    halo_xy = from_behind(tail_xy, "seq", 1)
    last = lax.optimization_barrier((d_low, d_high, tail_xy))
    proj_d, tail_d = project(last[:2], blocks, halo_rows)
    halo_d = from_behind(tail_d, "seq", 1)
    x_out, y_out = mix_packs(1, 3, *lax.optimization_barrier((proj_xy, halo_xy, tail_d))[:2])
    proj_d, halo_d, _ = lax.optimization_barrier((proj_d, halo_d, x_out))
    (d_out,) = mix_packs(3, 4, proj_d, halo_d)
    x_back, y_back, d_back = swap(x_out, 1), swap(y_out, 2), swap(d_out, 3)
    x_back, y_back = lax.optimization_barrier((x_back, y_back))
    total = total + jnp.dot(x_back, weights[1], preferred_element_type=jnp.float32)
    total = total + jnp.dot(y_back, weights[2], preferred_element_type=jnp.float32)
    (total,) = lax.optimization_barrier((total,))
    total = total + jnp.dot(d_back, weights[3], preferred_element_type=jnp.float32)
    return total.astype(jnp.bfloat16)


def solution(mesh):
    in_specs = (P(("fsdp", "seq"), None), P("fsdp", None), P(None, "fsdp"), P(), P(), P())
    out_specs = P(("fsdp", "seq"), None)
    body = local_four if mesh.shape["fsdp"] == 4 and mesh.shape["seq"] % 2 == 0 else local
    return jax.shard_map(body, mesh=mesh, in_specs=in_specs, out_specs=out_specs, check_vma=False)
```
